512 devices in a mesh: ctx: 64 (over y_hi, z, core), ch: 8 (over x, y_lo).
Axes of the slice: x: 4, y: 4 (y_hi: 2, y_lo: 2; y = y_hi * 2 + y_lo), z: 16, core: 2. Of those that a mesh axis runs over, the one named last changes fastest.
Arguments:
- tokens: bfloat16 [8192, 8192], P('ctx', 'ch'), may hold values from -6 to 6
- weights: bfloat16 [3, 8192, 512], P(None, 'ch'), may hold values from -0.0625 to 0.0625
- filter_taps: float32 [64, 8, 8192], P('ctx', 'ch'), may hold values from -32 to 32
- cotangent: bfloat16 [512, 8192], P('ch', 'ctx'), may hold values from -6 to 6
Outputs:
- gated_out: bfloat16 [512, 8192], P('ch', 'ctx')
- input_grad: bfloat16 [8192, 8192], P('ctx', 'ch')
- filter_grad: float32 [64, 8, 8192], P('ctx', 'ch')
The draws below stay inside these ranges and needn't reach their ends.
All inputs are finite; a program needn't handle non-finite values.
Results may differ from the reference program's by a relative error of at most 0.03.
Values may be sent and summed in bfloat16 or wider, within the bound.
No kernel may reach another device: no remote copies, remote signals or barrier semaphores. Data moves between devices by JAX's collectives and lax.ppermute only.
A program may use at most 64 MiB of HBM per device.

```python
import math
import jax
import jax.numpy as jnp
from jax import lax

D = 8192
C = 512
L = 8192
G = 8
CG = 64


def draw_filter_taps(key, part):
    key = jax.random.fold_in(key, 7)
    key_rate, key_noise, key_place, key_drop = jax.random.split(key, 4)
    length = L
    shape = (CG, G, length)
    low_rate = math.log(0.5 / length)
    high_rate = math.log(1.0 / 30.0)
    noise = jax.random.truncated_normal(key_noise, -4.0, 4.0, shape, jnp.float32)
    decay_rate = jnp.exp(jax.random.uniform(key_rate, (CG, G, 1), jnp.float32, low_rate, high_rate))
    coefficient_offset = lax.broadcasted_iota(jnp.int32, shape, 2)
    fading_profile = jnp.exp(-decay_rate * coefficient_offset.astype(jnp.float32))
    impulse_locations = jax.random.randint(key_place, (CG, G, 1, 3), 0, length)
    omitted_coefficients = jax.random.uniform(key_drop, (CG, G, 1, 3), jnp.float32, 0.5, 0.8)
    for surge_magnitude in range(3):
        fading_profile = fading_profile * jnp.where(coefficient_offset >= impulse_locations[:, :, :, surge_magnitude], omitted_coefficients[:, :, :, surge_magnitude], 1.0)
    energy = -jnp.expm1(-2.0 * decay_rate * length) / -jnp.expm1(-2.0 * decay_rate)
    amplitude = jnp.minimum(math.sqrt(length) / jnp.sqrt(energy), 8.0)
    return (noise * fading_profile * amplitude).astype(jnp.float32)


def steps_of(own_key, shape, pieces, least, top_value):
    gain = 1.0
    for axis_at, parts in pieces:
        steps = jax.random.uniform(jax.random.fold_in(jax.random.fold_in(own_key, 6), axis_at), (parts,), jnp.float32, least / len(pieces), top_value / len(pieces))
        gain = gain * jnp.repeat(jnp.exp(steps), shape[axis_at] // parts).reshape((-1,) + (1,) * (len(shape) - 1 - axis_at))
    return gain


def scatter_about(rng, shape, width, most, shards=(), dtype=jnp.bfloat16):
    level = steps_of(rng, shape, shards, -0.22, 0.18) if shards else 1.0
    drawn = jax.random.normal(rng, shape, jnp.float32) * width * level
    return jnp.minimum(jnp.maximum(drawn, -most), most).astype(dtype)


def setup_inputs(seed: int = 0) -> dict:
    splits = jax.random.split(jax.random.key(seed), 5)
    return {
        "tokens": scatter_about(splits[0], (L, D), 1.0, 6.0, ((0, 64), (1, 8))),
        "weights": scatter_about(splits[1], (3, D, C), D ** -0.5, 0.0625, ((1, 8),)),
        "filter_taps": draw_filter_taps(jax.random.fold_in(splits[4], 71), 0),
        "cotangent": scatter_about(splits[3], (C, L), 1.0, 6.0, ((0, 8), (1, 64))),
    }


def reference(tokens, weights, filter_taps, cotangent):
    group_width = D // G
    summed = jnp.zeros((3, C, L), jnp.float32)
    for group_index in range(G):
        low_edge = group_index * group_width
        part_tokens = tokens[:, low_edge:low_edge + group_width].astype(jnp.float32)
        part_weights = weights[:, low_edge:low_edge + group_width, :].astype(jnp.float32)
        partial_sum = jnp.einsum('sdc,td->sct', part_weights, part_tokens)
        rounded = lax.optimization_barrier(partial_sum.astype(jnp.bfloat16))
        summed = summed + rounded.astype(jnp.float32)
    projected = summed.astype(jnp.bfloat16)
    query = projected[0].astype(jnp.float32)
    keys_multiplier = projected[1].astype(jnp.float32)
    value_gate = projected[2].astype(jnp.float32)
    product = keys_multiplier * value_gate
    tap_scale = 1.0 / math.sqrt(L)
    kernel = jnp.transpose(filter_taps, (1, 0, 2)).reshape(C, L) * tap_scale
    padded_length = 2 * L
    prod_spec = jnp.fft.rfft(product, n=padded_length, axis=1)
    kernel_spec = jnp.fft.rfft(kernel, n=padded_length, axis=1)
    convolved = jnp.fft.irfft(prod_spec * kernel_spec, n=padded_length, axis=1)[:, :L]
    gated_out = (query * convolved).astype(jnp.bfloat16)
    upstream = cotangent.astype(jnp.float32)
    conv_grad = upstream * query
    query_grad = upstream * convolved
    grad_spec = jnp.fft.rfft(conv_grad, n=padded_length, axis=1)
    prod_grad = jnp.fft.irfft(grad_spec * jnp.conj(kernel_spec), n=padded_length, axis=1)[:, :L]
    kernel_grad = jnp.fft.irfft(grad_spec * jnp.conj(prod_spec), n=padded_length, axis=1)[:, :L] * tap_scale
    grads = jnp.stack([query_grad, prod_grad * value_gate, prod_grad * keys_multiplier]).astype(jnp.bfloat16)
    input_grad = jnp.einsum('sct,sdc->td', grads.astype(jnp.float32), weights.astype(jnp.float32)).astype(jnp.bfloat16)
    filter_grad = jnp.transpose(kernel_grad.reshape(G, CG, L), (1, 0, 2))
    return (gated_out, input_grad, filter_grad)
```

```python
import math

import jax
import jax.numpy as jnp
import numpy as np
from jax import lax
from jax.experimental import pallas as pl
from jax.experimental.pallas import tpu as pltpu
from jax.sharding import Mesh, PartitionSpec as P
import ml_dtypes

F32, BF16 = jnp.float32, jnp.bfloat16
SIDE = 128
LENGTH = 8192
BLOCKS = LENGTH // SIDE
YH, ZC, CH = 2, 32, 8
PLANE = CH * YH
SMALL = pltpu.CompilerParams(vmem_limit_bytes=8 * 1024 * 1024)


def halves(table):
    high = table.astype(ml_dtypes.bfloat16)
    low = (table - high.astype(np.float64)).astype(ml_dtypes.bfloat16)
    return high, low


def make_tables():
    index = np.arange(SIDE)
    angle = 2.0 * np.pi / SIDE * (np.outer(index, index) % SIDE)
    cos, sin = np.cos(angle), np.sin(angle)
    turn = 2.0 * np.pi / (SIDE * SIDE) * np.outer(index, index)
    twiddle = np.stack([np.cos(turn), np.sin(turn)]).astype(np.float32)
    zc, sig, yh = np.meshgrid(np.arange(ZC), np.arange(2), np.arange(YH), indexing="ij")
    block = (yh * ZC + zc).reshape(-1)
    sig = sig.reshape(-1)
    outer = np.concatenate([cos[:, block], -sin[:, block]], axis=0)
    outer = np.concatenate([outer * (sig == 0), outer * (sig == 1)], axis=0)
    outer = np.concatenate(halves(outer), axis=1)
    inner = np.stack(halves(np.block([[cos, -sin], [sin, cos]])))
    real_rows = np.concatenate([cos[block], -sin[block]], axis=1)
    imag_rows = np.concatenate([sin[block], cos[block]], axis=1)
    back = np.stack(halves(np.where((sig == 0)[:, None], real_rows, imag_rows)))
    plain = np.concatenate([cos[:, :BLOCKS], -sin[:, :BLOCKS]], axis=0)
    high, low = halves(plain)
    plain_outer = np.concatenate([high, low, high], axis=1)
    plain_back = np.stack(halves(np.concatenate([cos[:BLOCKS], -sin[:BLOCKS]], axis=1)))
    return outer, twiddle, inner, back, plain_outer, plain_back


def split(value):
    high = value.astype(BF16)
    return high, (value - high.astype(F32)).astype(BF16)


def mul(left, right, rhs_minor=False):
    dims = (((1,), (1 if rhs_minor else 0,)), ((), ()))
    return lax.dot_general(left, right, dims, preferred_element_type=F32)


def times_table(value, table, rhs_minor=False):
    high, low = split(value)
    return (
        mul(high, table[0], rhs_minor) + mul(low, table[0], rhs_minor) + mul(high, table[1], rhs_minor)
    )


def table_times(table, value):
    high, low = split(value)
    return mul(table[0], high) + mul(table[0], low) + mul(table[1], high)


def inner_forward(first, twiddle, inner):
    tc, ts = twiddle[0], twiddle[1]
    rows = []
    for s in range(first.shape[0] // (2 * SIDE)):
        re = first[2 * s * SIDE:(2 * s + 1) * SIDE]
        im = first[(2 * s + 1) * SIDE:(2 * s + 2) * SIDE]
        rows.append(jnp.concatenate([re * tc + im * ts, im * tc - re * ts], axis=1))
    stacked = rows[0] if len(rows) == 1 else jnp.concatenate(rows, axis=0)
    return times_table(stacked, inner)


def inner_backward(spec, twiddle, inner):
    tc, ts = twiddle[0], twiddle[1]
    mid = times_table(spec, inner, rhs_minor=True)
    re, im = mid[:, :SIDE], mid[:, SIDE:]
    return jnp.concatenate([re * tc - im * ts, im * tc + re * ts], axis=0)


def taps_kernel(taps_ref, plain_outer_ref, twiddle_ref, inner_ref, out_ref):
    scale = 1.0 / (math.sqrt(LENGTH) * SIDE * SIDE)
    high, low = split(taps_ref[...] * scale)
    first = mul(plain_outer_ref[...], jnp.concatenate([high, high, low], axis=0))
    out_ref[...] = inner_forward(first, twiddle_ref, inner_ref)


def gate_kernel(parts_ref, fields_ref, send_ref, scratch):
    mine = lax.axis_index("ch")
    for y in range(YH):
        fields = []
        for s in range(3):
            total = parts_ref[y, s].astype(F32)
            for g in range(1, CH):
                total = total + parts_ref[g * YH + y, s].astype(F32)
            rounded = total.astype(BF16)
            fields_ref[y, s] = rounded
            fields.append(rounded.astype(F32))
        upstream = parts_ref[mine * YH + y, 3]
        fields_ref[y, 3] = upstream
        scratch[pl.ds(y, ZC, stride=4), :] = fields[1] * fields[2]
        scratch[pl.ds(2 + y, ZC, stride=4), :] = upstream.astype(F32) * fields[0]
    send_ref[...] = scratch[...].astype(BF16)


def conv_kernel(rows_ref, taps_ref, outer_ref, twiddle_ref, inner_ref, back_ref, spec_ref, send_ref):
    rows = rows_ref[...]
    first = mul(outer_ref[...], jnp.concatenate([rows, rows], axis=0))
    spec = inner_forward(first, twiddle_ref, inner_ref)
    spec_ref[...] = spec
    pr, pi = spec[:SIDE, :SIDE], spec[:SIDE, SIDE:]
    gr, gi = spec[SIDE:, :SIDE], spec[SIDE:, SIDE:]
    kr, ki = taps_ref[:, :SIDE], taps_ref[:, SIDE:]
    re = pr * kr - pi * ki - (gi * kr - gr * ki)
    im = pr * ki + pi * kr + (gr * kr + gi * ki)
    mid = inner_backward(jnp.concatenate([re, im], axis=1), twiddle_ref, inner_ref)
    send_ref[...] = table_times(back_ref, mid).astype(BF16)


def filter_grad_kernel(spec_ref, twiddle_ref, inner_ref, plain_back_ref, out_ref):
    scale = 1.0 / (math.sqrt(LENGTH) * SIDE * SIDE)
    pr, pi = spec_ref[:SIDE, :SIDE], spec_ref[:SIDE, SIDE:]
    gr, gi = spec_ref[SIDE:, :SIDE], spec_ref[SIDE:, SIDE:]
    re = (gr * pr + gi * pi) * scale
    im = (gi * pr - gr * pi) * scale
    mid = inner_backward(jnp.concatenate([re, im], axis=1), twiddle_ref, inner_ref)
    out_ref[...] = table_times(plain_back_ref, mid)


def grads_kernel(rows_ref, fields_ref, send_ref, scratch):
    scratch[...] = rows_ref[...].astype(F32)
    for y in range(YH):
        convolved = scratch[pl.ds(y, ZC, stride=4), :]
        prod_grad = scratch[pl.ds(2 + y, ZC, stride=4), :]
        query, key, value, upstream = (fields_ref[y, s].astype(F32) for s in range(4))
        rows = (upstream * convolved, prod_grad * value, prod_grad * key, query * convolved)
        for s, row in enumerate(rows):
            row = row.astype(BF16)
            for g in range(CH):
                send_ref[g * YH + y, s] = row


def call(kernel, shapes, scratch=()):
    return pl.pallas_call(
        kernel,
        out_shape=shapes,
        compiler_params=SMALL,
        scratch_shapes=list(scratch),
    )


def shape(dims, dtype):
    return jax.ShapeDtypeStruct(dims, dtype)


def exchange(field, axes):
    return lax.all_to_all(field, axes, split_axis=0, concat_axis=0, tiled=True)


def on_device(tokens, weights, filter_taps, cotangent):
    outer, twiddle, inner, back, plain_outer, plain_back = (jnp.asarray(t) for t in make_tables())
    rows = SIDE
    parts = jnp.einsum(
        "sdpc,td->psct", weights.reshape(3, -1, PLANE, 32), tokens, preferred_element_type=F32
    ).astype(BF16)
    upstream = jnp.broadcast_to(
        cotangent.reshape(YH, 1, 32, rows)[None], (CH, YH, 1, 32, rows)
    ).reshape(PLANE, 1, 32, rows)
    parts = exchange(jnp.concatenate([parts, upstream], axis=1), ("ch", "yh"))
    taps = filter_taps.reshape(BLOCKS, SIDE)
    taps_spec = call(taps_kernel, shape((SIDE, 2 * SIDE), F32))(taps, plain_outer, twiddle, inner)
    fields, send = call(
        gate_kernel,
        (shape((YH, 4, 32, rows), BF16), shape((SIDE, SIDE), BF16)),
        [pltpu.VMEM((SIDE, SIDE), F32)],
    )(parts)
    arrived = exchange(send.reshape(ZC, 4, SIDE), "zc").reshape(SIDE, SIDE)
    spec, send = call(
        conv_kernel, (shape((2 * SIDE, 2 * SIDE), F32), shape((SIDE, SIDE), BF16))
    )(arrived, taps_spec, outer, twiddle, inner, back)
    arrived = exchange(send.reshape(ZC, 4, SIDE), "zc").reshape(SIDE, SIDE)
    kernel_grad = call(filter_grad_kernel, shape((BLOCKS, SIDE), F32))(
        spec, twiddle, inner, plain_back
    )
    grads = call(
        grads_kernel, shape((PLANE, 4, 32, rows), BF16), [pltpu.VMEM((SIDE, SIDE), F32)]
    )(arrived, fields)
    grads = exchange(grads, ("ch", "yh"))
    input_grad = jnp.einsum(
        "psct,sdpc->td",
        grads[:, :3],
        weights.reshape(3, -1, PLANE, 32),
        preferred_element_type=F32,
    ).astype(BF16)
    mine = lax.axis_index("ch")
    gated_out = lax.dynamic_slice_in_dim(grads[:, 3], mine * YH, YH, axis=0).reshape(2 * 32, rows)
    return gated_out, input_grad, kernel_grad.reshape(1, 1, LENGTH)


def solution(mesh):
    view = Mesh(mesh.devices.reshape(YH, ZC, CH), ("yh", "zc", "ch"))
    ctx = ("yh", "zc")
    return jax.shard_map(
        on_device,
        mesh=view,
        in_specs=(P(ctx, "ch"), P(None, "ch", None), P(ctx, "ch", None), P("ch", ctx)),
        out_specs=(P("ch", ctx), P(ctx, "ch"), P(ctx, "ch", None)),
        check_vma=False,
    )
```

```python
import math

import jax
import jax.numpy as jnp
import numpy as np
from jax import lax
from jax.experimental import pallas as pl
from jax.experimental.pallas import tpu as pltpu
from jax.sharding import Mesh, PartitionSpec as P
import ml_dtypes

F32, BF16 = jnp.float32, jnp.bfloat16
SIDE = 128
LENGTH = 8192
BLOCKS = LENGTH // SIDE
YH, ZC, CH = 2, 32, 8
PLANE = CH * YH
LARGE = pltpu.CompilerParams(vmem_limit_bytes=20 * 1024 * 1024)
SMALL = pltpu.CompilerParams(vmem_limit_bytes=8 * 1024 * 1024)


def halves(table):
    high = table.astype(ml_dtypes.bfloat16)
    low = (table - high.astype(np.float64)).astype(ml_dtypes.bfloat16)
    return high, low


def make_tables():
    index = np.arange(SIDE)
    angle = 2.0 * np.pi / SIDE * (np.outer(index, index) % SIDE)
    cos, sin = np.cos(angle), np.sin(angle)
    turn = 2.0 * np.pi / (SIDE * SIDE) * np.outer(index, index)
    twiddle = np.stack([np.cos(turn), np.sin(turn)]).astype(np.float32)
    zc, sig, yh = np.meshgrid(np.arange(ZC), np.arange(2), np.arange(YH), indexing="ij")
    block = (yh * ZC + zc).reshape(-1)
    sig = sig.reshape(-1)
    outer = np.concatenate([cos[:, block], -sin[:, block]], axis=0)
    outer = np.concatenate([outer * (sig == 0), outer * (sig == 1)], axis=0)
    outer = np.concatenate(halves(outer), axis=1)
    inner = np.stack(halves(np.block([[cos, -sin], [sin, cos]])))
    real_rows = np.concatenate([cos[block], -sin[block]], axis=1)
    imag_rows = np.concatenate([sin[block], cos[block]], axis=1)
    back = np.stack(halves(np.where((sig == 0)[:, None], real_rows, imag_rows)))
    plain = np.concatenate([cos[:, :BLOCKS], -sin[:, :BLOCKS]], axis=0)
    high, low = halves(plain)
    plain_outer = np.concatenate([high, low, high], axis=1)
    plain_back = np.stack(halves(np.concatenate([cos[:BLOCKS], -sin[:BLOCKS]], axis=1)))
    return outer, twiddle, inner, back, plain_outer, plain_back


def split(value):
    high = value.astype(BF16)
    return high, (value - high.astype(F32)).astype(BF16)


def mul(left, right, rhs_minor=False):
    dims = (((1,), (1 if rhs_minor else 0,)), ((), ()))
    return lax.dot_general(left, right, dims, preferred_element_type=F32)


def times_table(value, table, rhs_minor=False):
    high, low = split(value)
    return (
        mul(high, table[0], rhs_minor) + mul(low, table[0], rhs_minor) + mul(high, table[1], rhs_minor)
    )


def table_times(table, value):
    high, low = split(value)
    return mul(table[0], high) + mul(table[0], low) + mul(table[1], high)


def inner_forward(first, twiddle, inner):
    tc, ts = twiddle[0], twiddle[1]
    rows = []
    for s in range(first.shape[0] // (2 * SIDE)):
        re = first[2 * s * SIDE:(2 * s + 1) * SIDE]
        im = first[(2 * s + 1) * SIDE:(2 * s + 2) * SIDE]
        rows.append(jnp.concatenate([re * tc + im * ts, im * tc - re * ts], axis=1))
    stacked = rows[0] if len(rows) == 1 else jnp.concatenate(rows, axis=0)
    return times_table(stacked, inner)


def inner_backward(spec, twiddle, inner):
    tc, ts = twiddle[0], twiddle[1]
    mid = times_table(spec, inner, rhs_minor=True)
    re, im = mid[:, :SIDE], mid[:, SIDE:]
    return jnp.concatenate([re * tc - im * ts, im * tc + re * ts], axis=0)


def taps_spectrum(taps, plain_outer, twiddle, inner):
    scale = 1.0 / (math.sqrt(LENGTH) * SIDE * SIDE)
    high, low = split(taps * scale)
    first = mul(plain_outer, jnp.concatenate([high, high, low], axis=0))
    return inner_forward(first, twiddle, inner)


def project_kernel(*refs):
    sources, (send_ref, spec_ref), held, sems = refs[:7], refs[7:9], refs[9:16], refs[16]
    plain_outer, twiddle, inner, taps, cotangent, tokens, weights = held
    copies = [
        pltpu.make_async_copy(source, target, sems.at[i])
        for i, (source, target) in enumerate(zip(sources[:6], held[:6]))
    ] + [
        pltpu.make_async_copy(sources[6].at[s], weights.at[s], sems.at[6 + s]) for s in range(3)
    ]
    for copy in copies:
        copy.start()
    for copy in copies[:5]:
        copy.wait()
    for y in range(YH):
        upstream = cotangent[32 * y:32 * y + 32]
        for g in range(CH):
            send_ref[g * YH + y, 3] = upstream
    spec_ref[...] = taps_spectrum(taps[...], plain_outer[...], twiddle, inner)
    copies[5].wait()
    for s in range(3):
        copies[6 + s].wait()
        part = mul(tokens[...], weights[s]).T.astype(BF16)
        for p in range(PLANE):
            send_ref[p, s] = part[32 * p:32 * p + 32]


def gate_kernel(parts_ref, fields_ref, send_ref, scratch):
    mine = lax.axis_index("ch")
    for y in range(YH):
        fields = []
        for s in range(3):
            total = parts_ref[y, s].astype(F32)
            for g in range(1, CH):
                total = total + parts_ref[g * YH + y, s].astype(F32)
            rounded = total.astype(BF16)
            fields_ref[y, s] = rounded
            fields.append(rounded.astype(F32))
        upstream = parts_ref[mine * YH + y, 3]
        fields_ref[y, 3] = upstream
        scratch[pl.ds(y, ZC, stride=4), :] = fields[1] * fields[2]
        scratch[pl.ds(2 + y, ZC, stride=4), :] = upstream.astype(F32) * fields[0]
    send_ref[...] = scratch[...].astype(BF16)


def conv_kernel(rows_ref, taps_ref, outer_ref, twiddle_ref, inner_ref, back_ref, spec_ref, send_ref):
    rows = rows_ref[...]
    first = mul(outer_ref[...], jnp.concatenate([rows, rows], axis=0))
    spec = inner_forward(first, twiddle_ref, inner_ref)
    spec_ref[...] = spec
    pr, pi = spec[:SIDE, :SIDE], spec[:SIDE, SIDE:]
    gr, gi = spec[SIDE:, :SIDE], spec[SIDE:, SIDE:]
    kr, ki = taps_ref[:, :SIDE], taps_ref[:, SIDE:]
    re = pr * kr - pi * ki - (gi * kr - gr * ki)
    im = pr * ki + pi * kr + (gr * kr + gi * ki)
    mid = inner_backward(jnp.concatenate([re, im], axis=1), twiddle_ref, inner_ref)
    send_ref[...] = table_times(back_ref, mid).astype(BF16)


def filter_grad(spec_ref, twiddle_ref, inner_ref, plain_back_ref):
    scale = 1.0 / (math.sqrt(LENGTH) * SIDE * SIDE)
    pr, pi = spec_ref[:SIDE, :SIDE], spec_ref[:SIDE, SIDE:]
    gr, gi = spec_ref[SIDE:, :SIDE], spec_ref[SIDE:, SIDE:]
    re = (gr * pr + gi * pi) * scale
    im = (gi * pr - gr * pi) * scale
    mid = inner_backward(jnp.concatenate([re, im], axis=1), twiddle_ref, inner_ref)
    return table_times(plain_back_ref, mid)


def finish_kernel(
    grads_ref, weights_ref, spec_ref, twiddle_ref, inner_ref, plain_back_ref,
    gated_ref, input_ref, filter_ref,
):
    filter_ref[...] = filter_grad(spec_ref, twiddle_ref, inner_ref, plain_back_ref)
    mine = lax.axis_index("ch")
    for y in range(YH):
        gated_ref[32 * y:32 * y + 32] = grads_ref[mine * YH + y, 3]
    total = None
    for s in range(3):
        rows = jnp.concatenate([grads_ref[p, s] for p in range(PLANE)], axis=0)
        part = mul(rows.T, weights_ref[s], rhs_minor=True)
        total = part if total is None else total + part
    input_ref[...] = total.astype(BF16)


def grads_kernel(rows_ref, fields_ref, send_ref, scratch):
    scratch[...] = rows_ref[...].astype(F32)
    for y in range(YH):
        convolved = scratch[pl.ds(y, ZC, stride=4), :]
        prod_grad = scratch[pl.ds(2 + y, ZC, stride=4), :]
        query, key, value, upstream = (fields_ref[y, s].astype(F32) for s in range(4))
        rows = (upstream * convolved, prod_grad * value, prod_grad * key, query * convolved)
        for s, row in enumerate(rows):
            row = row.astype(BF16)
            for g in range(CH):
                send_ref[g * YH + y, s] = row


def call(kernel, shapes, scratch=(), params=SMALL, **extra):
    return pl.pallas_call(
        kernel, out_shape=shapes, compiler_params=params, scratch_shapes=list(scratch), **extra
    )


def shape(dims, dtype):
    return jax.ShapeDtypeStruct(dims, dtype)


def exchange(field, axes):
    return lax.all_to_all(field, axes, split_axis=0, concat_axis=0, tiled=True)


def on_device(tokens, weights, filter_taps, cotangent):
    outer, twiddle, inner, back, plain_outer, plain_back = (jnp.asarray(t) for t in make_tables())
    rows = SIDE
    operands = (
        plain_outer, twiddle, inner, filter_taps.reshape(BLOCKS, SIDE), cotangent, tokens, weights
    )
    parts, taps_spec = call(
        project_kernel,
        (pltpu.VMEM((PLANE, 4, 32, rows), BF16), pltpu.VMEM((SIDE, 2 * SIDE), F32)),
        [pltpu.VMEM(t.shape, t.dtype) for t in operands] + [pltpu.SemaphoreType.DMA((9,))],
        LARGE,
        in_specs=[pl.BlockSpec(memory_space=pltpu.HBM)] * 7,
    )(*(pltpu.with_memory_space_constraint(t, pltpu.HBM) for t in operands))
    parts = exchange(parts, ("ch", "yh"))
    fields, send = call(
        gate_kernel,
        (shape((YH, 4, 32, rows), BF16), shape((SIDE, SIDE), BF16)),
        [pltpu.VMEM((SIDE, SIDE), F32)],
    )(parts)
    arrived = exchange(send.reshape(ZC, 4, SIDE), "zc").reshape(SIDE, SIDE)
    spec, send = call(
        conv_kernel, (shape((2 * SIDE, 2 * SIDE), F32), shape((SIDE, SIDE), BF16))
    )(arrived, taps_spec, outer, twiddle, inner, back)
    arrived = exchange(send.reshape(ZC, 4, SIDE), "zc").reshape(SIDE, SIDE)
    grads = call(
        grads_kernel, shape((PLANE, 4, 32, rows), BF16), [pltpu.VMEM((SIDE, SIDE), F32)]
    )(arrived, fields)
    grads = exchange(grads, ("ch", "yh"))
    gated_out, input_grad, kernel_grad = call(
        finish_kernel,
        (shape((2 * 32, rows), BF16), shape(tokens.shape, BF16), shape((BLOCKS, SIDE), F32)),
    )(grads, weights, spec, twiddle, inner, plain_back)
    return gated_out, input_grad, kernel_grad.reshape(1, 1, LENGTH)


def solution(mesh):
    view = Mesh(mesh.devices.reshape(YH, ZC, CH), ("yh", "zc", "ch"))
    ctx = ("yh", "zc")
    return jax.shard_map(
        on_device,
        mesh=view,
        in_specs=(P(ctx, "ch"), P(None, "ch", None), P(ctx, "ch", None), P("ch", ctx)),
        out_specs=(P("ch", ctx), P(ctx, "ch"), P(ctx, "ch", None)),
        check_vma=False,
    )
```

```python
import math

import jax
import jax.numpy as jnp
import numpy as np
from jax import lax
from jax.experimental import pallas as pl
from jax.experimental.pallas import tpu as pltpu
from jax.sharding import PartitionSpec as P
import ml_dtypes

F32, BF16 = jnp.float32, jnp.bfloat16
SIDE = 128
LENGTH = 8192
BLOCKS = LENGTH // SIDE
CTX, CH = 64, 8
GROUP = 64


def led_by(first, size):
    order = list(range(size))
    order[0], order[first] = first, 0
    return order


CTX_FIRST, CH_FIRST = 54, 7
CTX_ORDER, CH_ORDER = led_by(CTX_FIRST, CTX), led_by(CH_FIRST, CH)
LARGE = pltpu.CompilerParams(vmem_limit_bytes=20 * 1024 * 1024)
SMALL = pltpu.CompilerParams(vmem_limit_bytes=8 * 1024 * 1024)


def halves(table):
    high = table.astype(ml_dtypes.bfloat16)
    low = (table - high.astype(np.float64)).astype(ml_dtypes.bfloat16)
    return high, low


def make_tables():
    index = np.arange(SIDE)
    angle = 2.0 * np.pi / SIDE * (np.outer(index, index) % SIDE)
    cos, sin = np.cos(angle), np.sin(angle)
    turn = 2.0 * np.pi / (SIDE * SIDE) * np.outer(index, index)
    twiddle = np.stack([np.cos(turn), np.sin(turn)]).astype(np.float32)
    block = np.repeat(np.array(CTX_ORDER), 2)
    sig = np.tile(np.arange(2), CTX)
    outer = np.concatenate([cos[:, block], -sin[:, block]], axis=0)
    outer = np.concatenate([outer * (sig == 0), outer * (sig == 1)], axis=0)
    outer = np.concatenate(halves(outer), axis=1)
    inner = np.stack(halves(np.block([[cos, -sin], [sin, cos]])))
    real_rows = np.concatenate([cos[block], -sin[block]], axis=1)
    imag_rows = np.concatenate([sin[block], cos[block]], axis=1)
    back = np.stack(halves(np.where((sig == 0)[:, None], real_rows, imag_rows)))
    plain = np.concatenate([cos[:, :BLOCKS], -sin[:, :BLOCKS]], axis=0)
    high, low = halves(plain)
    plain_outer = np.concatenate([high, low, high], axis=1)
    plain_back = np.stack(halves(np.concatenate([cos[:BLOCKS], -sin[:BLOCKS]], axis=1)))
    return outer, twiddle, inner, back, plain_outer, plain_back


def split(value):
    high = value.astype(BF16)
    return high, (value - high.astype(F32)).astype(BF16)


def mul(left, right, rhs_minor=False):
    dims = (((1,), (1 if rhs_minor else 0,)), ((), ()))
    return lax.dot_general(left, right, dims, preferred_element_type=F32)


def times_table(value, table, rhs_minor=False):
    high, low = split(value)
    return (
        mul(high, table[0], rhs_minor) + mul(low, table[0], rhs_minor) + mul(high, table[1], rhs_minor)
    )


def table_times(table, value):
    high, low = split(value)
    return mul(table[0], high) + mul(table[0], low) + mul(table[1], high)


def inner_forward(first, twiddle, inner):
    tc, ts = twiddle[0], twiddle[1]
    rows = []
    for s in range(first.shape[0] // (2 * SIDE)):
        re = first[2 * s * SIDE:(2 * s + 1) * SIDE]
        im = first[(2 * s + 1) * SIDE:(2 * s + 2) * SIDE]
        rows.append(jnp.concatenate([re * tc + im * ts, im * tc - re * ts], axis=1))
    stacked = rows[0] if len(rows) == 1 else jnp.concatenate(rows, axis=0)
    return times_table(stacked, inner)


def inner_backward(spec, twiddle, inner):
    tc, ts = twiddle[0], twiddle[1]
    mid = times_table(spec, inner, rhs_minor=True)
    re, im = mid[:, :SIDE], mid[:, SIDE:]
    return jnp.concatenate([re * tc - im * ts, im * tc + re * ts], axis=0)


def taps_spectrum(taps, plain_outer, twiddle, inner):
    scale = 1.0 / (math.sqrt(LENGTH) * SIDE * SIDE)
    high, low = split(taps * scale)
    first = mul(plain_outer, jnp.concatenate([high, high, low], axis=0))
    return inner_forward(first, twiddle, inner)


def project_kernel(*refs):
    sources, (send_ref, spec_ref, twiddle, inner, weights) = refs[:6], refs[6:11]
    plain_outer, taps, tokens, sems = refs[11:]
    held = (plain_outer, twiddle, inner, taps, tokens, weights)
    copies = [
        pltpu.make_async_copy(source, target, sems.at[i])
        for i, (source, target) in enumerate(zip(sources[:5], held[:5]))
    ] + [
        pltpu.make_async_copy(sources[5].at[s], weights.at[s], sems.at[5 + s]) for s in range(3)
    ]
    for copy in copies:
        copy.start()
    for copy in copies[:4]:
        copy.wait()
    spec_ref[...] = taps_spectrum(taps[...], plain_outer[...], twiddle, inner)
    copies[4].wait()
    for s in range(3):
        copies[5 + s].wait()
        part = mul(tokens[...], weights[s]).T.astype(BF16)
        for k, g in enumerate(CH_ORDER):
            send_ref[k, s] = part[GROUP * g:GROUP * (g + 1)]


def swap_peers(rows_ref):
    far = pl.ds(2 * CTX_FIRST, 2)
    first, other = rows_ref[0:2], rows_ref[far]
    rows_ref[0:2] = other
    rows_ref[far] = first


def gate_kernel(parts_ref, cotangent_ref, fields_ref, send_ref, scratch):
    fields = []
    for s in range(3):
        total = parts_ref[0, s].astype(F32)
        for g in range(1, CH):
            total = total + parts_ref[g, s].astype(F32)
        rounded = total.astype(BF16)
        fields_ref[s] = rounded
        fields.append(rounded.astype(F32))
    scratch[pl.ds(0, CTX, stride=2), :] = fields[1] * fields[2]
    scratch[pl.ds(1, CTX, stride=2), :] = cotangent_ref[...].astype(F32) * fields[0]
    swap_peers(scratch)
    send_ref[...] = scratch[...].astype(BF16)


def conv_kernel(rows_ref, taps_ref, outer_ref, twiddle_ref, inner_ref, back_ref, spec_ref, send_ref):
    rows = rows_ref[...]
    first = mul(outer_ref[...], jnp.concatenate([rows, rows], axis=0))
    spec = inner_forward(first, twiddle_ref, inner_ref)
    spec_ref[...] = spec
    pr, pi = spec[:SIDE, :SIDE], spec[:SIDE, SIDE:]
    gr, gi = spec[SIDE:, :SIDE], spec[SIDE:, SIDE:]
    kr, ki = taps_ref[:, :SIDE], taps_ref[:, SIDE:]
    re = pr * kr - pi * ki - (gi * kr - gr * ki)
    im = pr * ki + pi * kr + (gr * kr + gi * ki)
    mid = inner_backward(jnp.concatenate([re, im], axis=1), twiddle_ref, inner_ref)
    send_ref[...] = table_times(back_ref, mid).astype(BF16)


def filter_grad(spec_ref, twiddle_ref, inner_ref, plain_back_ref):
    scale = 1.0 / (math.sqrt(LENGTH) * SIDE * SIDE)
    pr, pi = spec_ref[:SIDE, :SIDE], spec_ref[:SIDE, SIDE:]
    gr, gi = spec_ref[SIDE:, :SIDE], spec_ref[SIDE:, SIDE:]
    re = (gr * pr + gi * pi) * scale
    im = (gi * pr - gr * pi) * scale
    mid = inner_backward(jnp.concatenate([re, im], axis=1), twiddle_ref, inner_ref)
    return table_times(plain_back_ref, mid)


def finish_kernel(
    grads_ref, gated_in_ref, weights_ref, spec_ref, twiddle_ref, inner_ref, plain_back_ref,
    gated_ref, input_ref, filter_ref,
):
    gated_ref[...] = gated_in_ref[...]
    filter_ref[...] = filter_grad(spec_ref, twiddle_ref, inner_ref, plain_back_ref)
    total = None
    for s in range(3):
        rows = jnp.concatenate([grads_ref[CH_ORDER.index(g), s] for g in range(CH)], axis=0)
        part = mul(rows.T, weights_ref[s], rhs_minor=True)
        total = part if total is None else total + part
    input_ref[...] = total.astype(BF16)


def grads_kernel(rows_ref, fields_ref, cotangent_ref, send_ref, gated_ref, scratch):
    scratch[...] = rows_ref[...].astype(F32)
    swap_peers(scratch)
    convolved = scratch[pl.ds(0, CTX, stride=2), :]
    prod_grad = scratch[pl.ds(1, CTX, stride=2), :]
    query, key, value = (fields_ref[s].astype(F32) for s in range(3))
    upstream = cotangent_ref[...].astype(F32)
    gated_ref[...] = (query * convolved).astype(BF16)
    for s, row in enumerate((upstream * convolved, prod_grad * value, prod_grad * key)):
        row = row.astype(BF16)
        for k in range(CH):
            send_ref[k, s] = row


def call(kernel, shapes, scratch=(), params=SMALL, **extra):
    return pl.pallas_call(
        kernel, out_shape=shapes, compiler_params=params, scratch_shapes=list(scratch), **extra
    )


def shape(dims, dtype):
    return jax.ShapeDtypeStruct(dims, dtype)


def exchange(field, axis, order):
    return lax.all_to_all(
        field, axis, split_axis=0, concat_axis=0, tiled=True, axis_index_groups=[list(order)]
    )


def over_ctx(rows):
    return exchange(rows.reshape(CTX, 2, SIDE), "ctx", CTX_ORDER).reshape(SIDE, SIDE)


def on_device(tokens, weights, filter_taps, cotangent):
    outer, twiddle, inner, back, plain_outer, plain_back = (jnp.asarray(t) for t in make_tables())
    message = (CH, 3, GROUP, SIDE)
    operands = (plain_outer, twiddle, inner, filter_taps.reshape(BLOCKS, SIDE), tokens, weights)
    kept = (twiddle, inner, weights)
    parts, taps_spec, twiddle, inner, weights = call(
        project_kernel,
        (pltpu.VMEM(message, BF16), pltpu.VMEM((SIDE, 2 * SIDE), F32))
        + tuple(pltpu.VMEM(t.shape, t.dtype) for t in kept),
        [pltpu.VMEM(operands[i].shape, operands[i].dtype) for i in (0, 3, 4)]
        + [pltpu.SemaphoreType.DMA((8,))],
        LARGE,
        in_specs=[pl.BlockSpec(memory_space=pltpu.HBM)] * 6,
    )(*(pltpu.with_memory_space_constraint(t, pltpu.HBM) for t in operands))
    parts = exchange(parts, "ch", CH_ORDER)
    fields, send = call(
        gate_kernel,
        (shape((3, GROUP, SIDE), BF16), shape((SIDE, SIDE), BF16)),
        [pltpu.VMEM((SIDE, SIDE), F32)],
    )(parts, cotangent)
    spec, send = call(
        conv_kernel, (shape((2 * SIDE, 2 * SIDE), F32), shape((SIDE, SIDE), BF16))
    )(over_ctx(send), taps_spec, outer, twiddle, inner, back)
    grads, gated = call(
        grads_kernel,
        (shape(message, BF16), shape((GROUP, SIDE), BF16)),
        [pltpu.VMEM((SIDE, SIDE), F32)],
    )(over_ctx(send), fields, cotangent)
    grads = exchange(grads, "ch", CH_ORDER)
    gated_out, input_grad, kernel_grad = call(
        finish_kernel,
        (
            shape((GROUP, SIDE), BF16),
            shape(tokens.shape, BF16),
            shape((BLOCKS, SIDE), F32),
        ),
    )(grads, gated, weights, spec, twiddle, inner, plain_back)
    return gated_out, input_grad, kernel_grad.reshape(1, 1, LENGTH)


def solution(mesh):
    return jax.shard_map(
        on_device,
        mesh=mesh,
        in_specs=(P("ctx", "ch"), P(None, "ch", None), P("ctx", "ch", None), P("ch", "ctx")),
        out_specs=(P("ch", "ctx"), P("ctx", "ch"), P("ctx", "ch", None)),
        check_vma=False,
    )
```

```python
import math

import jax
import jax.numpy as jnp
import numpy as np
from jax import lax
from jax.experimental import pallas as pl
from jax.experimental.pallas import tpu as pltpu
from jax.sharding import PartitionSpec as P
import ml_dtypes

F32, BF16 = jnp.float32, jnp.bfloat16
SIDE = 128
LENGTH = 8192
BLOCKS = LENGTH // SIDE
CTX, CH = 64, 8
GROUP = 64


def led_by(first, size):
    order = list(range(size))
    order[0], order[first] = first, 0
    return order


CTX_FIRST, CH_FIRST = 54, 7
CTX_ORDER, CH_ORDER = led_by(CTX_FIRST, CTX), led_by(CH_FIRST, CH)
LARGE = pltpu.CompilerParams(vmem_limit_bytes=20 * 1024 * 1024)
SMALL = pltpu.CompilerParams(vmem_limit_bytes=8 * 1024 * 1024)


def halves(table):
    high = table.astype(ml_dtypes.bfloat16)
    low = (table - high.astype(np.float64)).astype(ml_dtypes.bfloat16)
    return high, low


def make_tables():
    index = np.arange(SIDE)
    angle = 2.0 * np.pi / SIDE * (np.outer(index, index) % SIDE)
    cos, sin = np.cos(angle), np.sin(angle)
    turn = 2.0 * np.pi / (SIDE * SIDE) * np.outer(index, index)
    twiddle = np.stack([np.cos(turn), np.sin(turn)]).astype(np.float32)
    block = np.repeat(np.array(CTX_ORDER), 2)
    sig = np.tile(np.arange(2), CTX)
    outer = np.concatenate([cos[:, block], -sin[:, block]], axis=0)
    outer = np.concatenate([outer * (sig == 0), outer * (sig == 1)], axis=0)
    outer = np.concatenate(halves(outer), axis=1)
    inner = np.stack(halves(np.block([[cos, -sin], [sin, cos]])))
    real_rows = np.concatenate([cos[block], -sin[block]], axis=1)
    imag_rows = np.concatenate([sin[block], cos[block]], axis=1)
    back = np.stack(halves(np.where((sig == 0)[:, None], real_rows, imag_rows)))
    plain = np.concatenate([cos[:, :BLOCKS], -sin[:, :BLOCKS]], axis=0)
    high, low = halves(plain)
    plain_outer = np.concatenate([high, low, high], axis=1)
    plain_back = np.stack(halves(np.concatenate([cos[:BLOCKS], -sin[:BLOCKS]], axis=1)))
    return outer, twiddle, inner, back, plain_outer, plain_back


def split(value):
    high = value.astype(BF16)
    return high, (value - high.astype(F32)).astype(BF16)


def mul(left, right, rhs_minor=False):
    dims = (((1,), (1 if rhs_minor else 0,)), ((), ()))
    return lax.dot_general(left, right, dims, preferred_element_type=F32)


def times_table(value, table, rhs_minor=False):
    high, low = split(value)
    return (
        mul(high, table[0], rhs_minor) + mul(low, table[0], rhs_minor) + mul(high, table[1], rhs_minor)
    )


def table_times(table, value):
    high, low = split(value)
    return mul(table[0], high) + mul(table[0], low) + mul(table[1], high)


def inner_forward(first, twiddle, inner):
    tc, ts = twiddle[0], twiddle[1]
    rows = []
    for s in range(first.shape[0] // (2 * SIDE)):
        re = first[2 * s * SIDE:(2 * s + 1) * SIDE]
        im = first[(2 * s + 1) * SIDE:(2 * s + 2) * SIDE]
        rows.append(jnp.concatenate([re * tc + im * ts, im * tc - re * ts], axis=1))
    stacked = rows[0] if len(rows) == 1 else jnp.concatenate(rows, axis=0)
    return times_table(stacked, inner)


def turn_back(mid, twiddle):
    tc, ts = twiddle[0], twiddle[1]
    re, im = mid[:, :SIDE], mid[:, SIDE:]
    return jnp.concatenate([re * tc - im * ts, im * tc + re * ts], axis=0)


def project_kernel(tokens_hbm, weights_hbm, send_ref, weights, tokens, sems):
    half = weights.shape[1] // 2
    parts = [pl.ds(h * half, half) for h in range(2)]
    tokens_copy = pltpu.make_async_copy(tokens_hbm, tokens, sems.at[6])
    tokens_copy.start()
    blocks = [
        pltpu.make_async_copy(
            weights_hbm.at[i // 2, parts[i % 2]], weights.at[i // 2, parts[i % 2]], sems.at[i]
        )
        for i in range(6)
    ]
    for copy in blocks:
        copy.start()
    tokens_copy.wait()
    for s in range(3):
        total = None
        for h in range(2):
            blocks[2 * s + h].wait()
            part = mul(tokens[:, half * h:half * (h + 1)], weights[s, half * h:half * (h + 1)])
            total = part if total is None else total + part
        total = total.astype(BF16).T
        for k, g in enumerate(CH_ORDER):
            send_ref[k, s] = total[GROUP * g:GROUP * (g + 1)]


def swap_peers(rows_ref):
    far = pl.ds(2 * CTX_FIRST, 2)
    first, other = rows_ref[0:2], rows_ref[far]
    rows_ref[0:2] = other
    rows_ref[far] = first


def gate_kernel(parts_ref, cotangent_ref, fields_ref, send_ref, scratch):
    fields = []
    for s in range(3):
        total = parts_ref[0, s].astype(F32)
        for g in range(1, CH):
            total = total + parts_ref[g, s].astype(F32)
        rounded = total.astype(BF16)
        fields_ref[s] = rounded
        fields.append(rounded.astype(F32))
    scratch[pl.ds(0, CTX, stride=2), :] = fields[1] * fields[2]
    scratch[pl.ds(1, CTX, stride=2), :] = cotangent_ref[...].astype(F32) * fields[0]
    swap_peers(scratch)
    send_ref[...] = scratch[...].astype(BF16)


def conv_kernel(
    rows_ref, taps_ref, outer_ref, plain_outer_ref, twiddle_ref, inner_ref, back_ref,
    plain_back_ref, filter_ref, send_ref,
):
    rows = rows_ref[...]
    high, low = split(taps_ref[...] * (1.0 / (math.sqrt(LENGTH) * SIDE * SIDE)))
    taps = mul(plain_outer_ref[...], jnp.concatenate([high, high, low], axis=0))
    first = mul(outer_ref[...], jnp.concatenate([rows, rows], axis=0))
    spec = inner_forward(jnp.concatenate([first, taps], axis=0), twiddle_ref, inner_ref)
    (pr, pi), (gr, gi), (kr, ki) = (
        (spec[s * SIDE:(s + 1) * SIDE, :SIDE], spec[s * SIDE:(s + 1) * SIDE, SIDE:])
        for s in range(3)
    )
    re = pr * kr - pi * ki - (gi * kr - gr * ki)
    im = pr * ki + pi * kr + (gr * kr + gi * ki)
    scale = 1.0 / (math.sqrt(LENGTH) * SIDE * SIDE)
    filter_re = (gr * pr + gi * pi) * scale
    filter_im = (gi * pr - gr * pi) * scale
    both = jnp.concatenate(
        [
            jnp.concatenate([re, im], axis=1),
            jnp.concatenate([filter_re, filter_im], axis=1),
        ],
        axis=0,
    )
    mid = times_table(both, inner_ref, rhs_minor=True)
    send_ref[...] = table_times(back_ref, turn_back(mid[:SIDE], twiddle_ref)).astype(BF16)
    filter_ref[...] = table_times(plain_back_ref, turn_back(mid[SIDE:], twiddle_ref))


def finish_kernel(
    grads_ref, gated_in_ref, filter_in_ref, weights_ref, gated_ref, input_ref, filter_ref
):
    gated_ref[...] = gated_in_ref[...]
    filter_ref[...] = filter_in_ref[...]
    total = None
    for s in range(3):
        rows = jnp.concatenate([grads_ref[CH_ORDER.index(g), s] for g in range(CH)], axis=0)
        part = mul(weights_ref[s], rows)
        total = part if total is None else total + part
    input_ref[...] = total.astype(BF16).T


def grads_kernel(rows_ref, fields_ref, cotangent_ref, send_ref, gated_ref, scratch):
    scratch[...] = rows_ref[...].astype(F32)
    swap_peers(scratch)
    convolved = scratch[pl.ds(0, CTX, stride=2), :]
    prod_grad = scratch[pl.ds(1, CTX, stride=2), :]
    query, key, value = (fields_ref[s].astype(F32) for s in range(3))
    upstream = cotangent_ref[...].astype(F32)
    gated_ref[...] = (query * convolved).astype(BF16)
    for s, row in enumerate((upstream * convolved, prod_grad * value, prod_grad * key)):
        row = row.astype(BF16)
        for k in range(CH):
            send_ref[k, s] = row


def call(kernel, shapes, scratch=(), params=SMALL, **extra):
    return pl.pallas_call(
        kernel, out_shape=shapes, compiler_params=params, scratch_shapes=list(scratch), **extra
    )


def shape(dims, dtype):
    return jax.ShapeDtypeStruct(dims, dtype)


def exchange(field, axis, order):
    return lax.all_to_all(
        field, axis, split_axis=0, concat_axis=0, tiled=True, axis_index_groups=[list(order)]
    )


def over_ctx(rows):
    return exchange(rows.reshape(CTX, 2, SIDE), "ctx", CTX_ORDER).reshape(SIDE, SIDE)


def on_device(tokens, weights, filter_taps, cotangent):
    tables = [jnp.asarray(t) for t in make_tables()]
    message = (CH, 3, GROUP, SIDE)
    parts, weights = call(
        project_kernel,
        (pltpu.VMEM(message, BF16), pltpu.VMEM(weights.shape, BF16)),
        [pltpu.VMEM(tokens.shape, BF16), pltpu.SemaphoreType.DMA((7,))],
        LARGE,
        in_specs=[pl.BlockSpec(memory_space=pltpu.HBM)] * 2,
    )(*(pltpu.with_memory_space_constraint(t, pltpu.HBM) for t in (tokens, weights)))
    taps = filter_taps.reshape(BLOCKS, SIDE)
    parts, taps, cotangent, *tables = lax.optimization_barrier((parts, taps, cotangent, *tables))
    outer, twiddle, inner, back, plain_outer, plain_back = tables
    parts = exchange(parts, "ch", CH_ORDER)
    fields, send = call(
        gate_kernel,
        (shape((3, GROUP, SIDE), BF16), shape((SIDE, SIDE), BF16)),
        [pltpu.VMEM((SIDE, SIDE), F32)],
    )(parts, cotangent)
    kernel_grad, send = call(
        conv_kernel, (shape((BLOCKS, SIDE), F32), shape((SIDE, SIDE), BF16))
    )(over_ctx(send), taps, outer, plain_outer, twiddle, inner, back, plain_back)
    grads, gated = call(
        grads_kernel,
        (shape(message, BF16), shape((GROUP, SIDE), BF16)),
        [pltpu.VMEM((SIDE, SIDE), F32)],
    )(over_ctx(send), fields, cotangent)
    grads = exchange(grads, "ch", CH_ORDER)
    gated_out, input_grad, kernel_grad = call(
        finish_kernel,
        (
            shape((GROUP, SIDE), BF16),
            shape(tokens.shape, BF16),
            shape((BLOCKS, SIDE), F32),
        ),
    )(grads, gated, kernel_grad, weights)
    return gated_out, input_grad, kernel_grad.reshape(1, 1, LENGTH)


def solution(mesh):
    return jax.shard_map(
        on_device,
        mesh=mesh,
        in_specs=(P("ctx", "ch"), P(None, "ch", None), P("ctx", "ch", None), P("ch", "ctx")),
        out_specs=(P("ch", "ctx"), P("ctx", "ch"), P("ctx", "ch", None)),
        check_vma=False,
    )
```

```python
import math

import jax
import jax.numpy as jnp
import numpy as np
from jax import lax
from jax.experimental import pallas as pl
from jax.experimental.pallas import tpu as pltpu
from jax.sharding import PartitionSpec as P
import ml_dtypes

F32, BF16 = jnp.float32, jnp.bfloat16
SIDE = 128
LENGTH = 8192
BLOCKS = LENGTH // SIDE
CTX, CH = 64, 8
GROUP = 64


def led_by(first, size):
    order = list(range(size))
    order[0], order[first] = first, 0
    return order


CTX_FIRST, CH_FIRST = 53, 7
CTX_ORDER, CH_ORDER = led_by(CTX_FIRST, CTX), led_by(CH_FIRST, CH)
LARGE = pltpu.CompilerParams(vmem_limit_bytes=20 * 1024 * 1024)
SMALL = pltpu.CompilerParams(vmem_limit_bytes=8 * 1024 * 1024)


def halves(table):
    high = table.astype(ml_dtypes.bfloat16)
    low = (table - high.astype(np.float64)).astype(ml_dtypes.bfloat16)
    return high, low


def make_tables():
    index = np.arange(SIDE)
    angle = 2.0 * np.pi / SIDE * (np.outer(index, index) % SIDE)
    waves = np.stack(halves(np.cos(angle)) + halves(np.sin(angle)))
    turn = 2.0 * np.pi / (SIDE * SIDE) * np.outer(index, index)
    twiddle = np.stack([np.cos(turn), np.sin(turn)]).astype(np.float32)
    return waves, twiddle


def split(value):
    high = value.astype(BF16)
    return high, (value - high.astype(F32)).astype(BF16)


def mul(left, right, rhs_minor=False):
    dims = (((1,), (1 if rhs_minor else 0,)), ((), ()))
    return lax.dot_general(left, right, dims, preferred_element_type=F32)


def times_table(value, table, rhs_minor=False):
    high, low = split(value)
    return (
        mul(high, table[0], rhs_minor) + mul(low, table[0], rhs_minor) + mul(high, table[1], rhs_minor)
    )


def table_times(table, value):
    high, low = split(value)
    return mul(table[0], high) + mul(table[0], low) + mul(table[1], high)


def block(rows):
    return jnp.concatenate([jnp.concatenate(row, axis=1) for row in rows], axis=0)


def turn_back(mid, twiddle):
    tc, ts = twiddle[0], twiddle[1]
    re, im = mid[:, :SIDE], mid[:, SIDE:]
    return jnp.concatenate([re * tc - im * ts, im * tc + re * ts], axis=0)


def project_kernel(tokens_hbm, weights_hbm, send_ref, weights, tokens, sems):
    half = weights.shape[1] // 2
    parts = [pl.ds(h * half, half) for h in range(2)]
    tokens_copy = pltpu.make_async_copy(tokens_hbm, tokens, sems.at[6])
    tokens_copy.start()
    blocks = [
        pltpu.make_async_copy(
            weights_hbm.at[i // 2, parts[i % 2]], weights.at[i // 2, parts[i % 2]], sems.at[i]
        )
        for i in range(6)
    ]
    for copy in blocks:
        copy.start()
    tokens_copy.wait()
    for s in range(3):
        total = None
        for h in range(2):
            blocks[2 * s + h].wait()
            part = mul(tokens[:, half * h:half * (h + 1)], weights[s, half * h:half * (h + 1)])
            total = part if total is None else total + part
        total = total.astype(BF16).T
        for k, g in enumerate(CH_ORDER):
            send_ref[k, s] = total[GROUP * g:GROUP * (g + 1)]


def swap_peers(rows_ref):
    far = pl.ds(2 * CTX_FIRST, 2)
    first, other = rows_ref[0:2], rows_ref[far]
    rows_ref[0:2] = other
    rows_ref[far] = first


def gate_kernel(parts_ref, cotangent_ref, fields_ref, send_ref, scratch):
    fields = []
    for s in range(3):
        total = parts_ref[0, s].astype(F32)
        for g in range(1, CH):
            total = total + parts_ref[g, s].astype(F32)
        rounded = total.astype(BF16)
        fields_ref[s] = rounded
        fields.append(rounded.astype(F32))
    scratch[pl.ds(0, CTX, stride=2), :] = fields[1] * fields[2]
    scratch[pl.ds(1, CTX, stride=2), :] = cotangent_ref[...].astype(F32) * fields[0]
    swap_peers(scratch)
    send_ref[...] = scratch[...].astype(BF16)


def conv_kernel(rows_ref, taps_ref, waves_ref, twiddle_ref, filter_ref, send_ref, scratch):
    cos, sin = (waves_ref[0], waves_ref[1]), (waves_ref[2], waves_ref[3])
    tc, ts = twiddle_ref[0], twiddle_ref[1]
    scratch[...] = rows_ref[...].astype(F32)
    swap_peers(scratch)
    product = scratch[pl.ds(0, CTX, stride=2), :].astype(BF16)
    conv_grad = scratch[pl.ds(1, CTX, stride=2), :].astype(BF16)
    high, low = split(taps_ref[...] * (1.0 / (math.sqrt(LENGTH) * SIDE * SIDE)))
    signals = jnp.concatenate([product, conv_grad, high], axis=1)
    signals = jnp.concatenate([signals, jnp.zeros_like(signals)], axis=0)
    outer = [jnp.concatenate([cos[i], -sin[i]], axis=0) for i in range(2)]
    first = mul(jnp.concatenate(outer, axis=1), jnp.concatenate([signals, signals], axis=0))
    rest = mul(outer[0], jnp.concatenate([low, jnp.zeros_like(low)], axis=0))
    turned = []
    for s in range(3):
        part = first[:, s * SIDE:(s + 1) * SIDE]
        if s == 2:
            part = part + rest
        re, im = part[:SIDE], part[SIDE:]
        turned.append(jnp.concatenate([re * tc + im * ts, im * tc - re * ts], axis=1))
    inner = [block([[cos[i], -sin[i]], [sin[i], cos[i]]]) for i in range(2)]
    spec = times_table(jnp.concatenate(turned, axis=0), inner)
    (pr, pi), (gr, gi), (kr, ki) = (
        (spec[s * SIDE:(s + 1) * SIDE, :SIDE], spec[s * SIDE:(s + 1) * SIDE, SIDE:])
        for s in range(3)
    )
    re = pr * kr - pi * ki - (gi * kr - gr * ki)
    im = pr * ki + pi * kr + (gr * kr + gi * ki)
    scale = 1.0 / (math.sqrt(LENGTH) * SIDE * SIDE)
    filter_re = (gr * pr + gi * pi) * scale
    filter_im = (gi * pr - gr * pi) * scale
    mid = times_table(block([[re, im], [filter_re, filter_im]]), inner, rhs_minor=True)
    back = [
        block([[cos[i][:BLOCKS], -sin[i][:BLOCKS]], [sin[i][:BLOCKS], cos[i][:BLOCKS]]])
        for i in range(2)
    ]
    both = table_times(back, turn_back(mid[:SIDE], twiddle_ref))
    scratch[pl.ds(0, CTX, stride=2), :] = both[:BLOCKS]
    scratch[pl.ds(1, CTX, stride=2), :] = both[BLOCKS:]
    swap_peers(scratch)
    send_ref[...] = scratch[...].astype(BF16)
    filter_ref[...] = table_times(
        [part[:BLOCKS] for part in back], turn_back(mid[SIDE:], twiddle_ref)
    )


def finish_kernel(
    grads_ref, gated_in_ref, filter_in_ref, weights_ref, gated_ref, input_ref, filter_ref
):
    gated_ref[...] = gated_in_ref[...]
    filter_ref[...] = filter_in_ref[...]
    total = None
    for s in range(3):
        rows = jnp.concatenate([grads_ref[CH_ORDER.index(g), s] for g in range(CH)], axis=0)
        part = mul(weights_ref[s], rows)
        total = part if total is None else total + part
    input_ref[...] = total.astype(BF16).T


def grads_kernel(rows_ref, fields_ref, cotangent_ref, send_ref, gated_ref, scratch):
    scratch[...] = rows_ref[...].astype(F32)
    swap_peers(scratch)
    convolved = scratch[pl.ds(0, CTX, stride=2), :]
    prod_grad = scratch[pl.ds(1, CTX, stride=2), :]
    query, key, value = (fields_ref[s].astype(F32) for s in range(3))
    upstream = cotangent_ref[...].astype(F32)
    gated_ref[...] = (query * convolved).astype(BF16)
    for s, row in enumerate((upstream * convolved, prod_grad * value, prod_grad * key)):
        row = row.astype(BF16)
        for k in range(CH):
            send_ref[k, s] = row


def call(kernel, shapes, scratch=(), params=SMALL, **extra):
    return pl.pallas_call(
        kernel, out_shape=shapes, compiler_params=params, scratch_shapes=list(scratch), **extra
    )


def shape(dims, dtype):
    return jax.ShapeDtypeStruct(dims, dtype)


def exchange(field, axis, order):
    return lax.all_to_all(
        field, axis, split_axis=0, concat_axis=0, tiled=True, axis_index_groups=[list(order)]
    )


def over_ctx(rows):
    return exchange(rows.reshape(CTX, 2, SIDE), "ctx", CTX_ORDER).reshape(SIDE, SIDE)


def on_device(tokens, weights, filter_taps, cotangent):
    waves, twiddle = (jnp.asarray(t) for t in make_tables())
    message = (CH, 3, GROUP, SIDE)
    parts, weights = call(
        project_kernel,
        (pltpu.VMEM(message, BF16), pltpu.VMEM(weights.shape, BF16)),
        [pltpu.VMEM(tokens.shape, BF16), pltpu.SemaphoreType.DMA((7,))],
        LARGE,
        in_specs=[pl.BlockSpec(memory_space=pltpu.HBM)] * 2,
    )(*(pltpu.with_memory_space_constraint(t, pltpu.HBM) for t in (tokens, weights)))
    parts = exchange(parts, "ch", CH_ORDER)
    fields, send = call(
        gate_kernel,
        (shape((3, GROUP, SIDE), BF16), shape((SIDE, SIDE), BF16)),
        [pltpu.VMEM((SIDE, SIDE), F32)],
    )(parts, cotangent)
    kernel_grad, send = call(
        conv_kernel,
        (shape((BLOCKS, SIDE), F32), shape((SIDE, SIDE), BF16)),
        [pltpu.VMEM((SIDE, SIDE), F32)],
    )(over_ctx(send), filter_taps.reshape(BLOCKS, SIDE), waves, twiddle)
    grads, gated = call(
        grads_kernel,
        (shape(message, BF16), shape((GROUP, SIDE), BF16)),
        [pltpu.VMEM((SIDE, SIDE), F32)],
    )(over_ctx(send), fields, cotangent)
    grads = exchange(grads, "ch", CH_ORDER)
    gated_out, input_grad, kernel_grad = call(
        finish_kernel,
        (
            shape((GROUP, SIDE), BF16),
            shape(tokens.shape, BF16),
            shape((BLOCKS, SIDE), F32),
        ),
    )(grads, gated, kernel_grad, weights)
    return gated_out, input_grad, kernel_grad.reshape(1, 1, LENGTH)


def solution(mesh):
    return jax.shard_map(
        on_device,
        mesh=mesh,
        in_specs=(P("ctx", "ch"), P(None, "ch", None), P("ctx", "ch", None), P("ch", "ctx")),
        out_specs=(P("ch", "ctx"), P("ctx", "ch"), P("ctx", "ch", None)),
        check_vma=False,
    )
```

```python
import math

import jax
import jax.numpy as jnp
import numpy as np
from jax import lax
from jax.experimental import pallas as pl
from jax.experimental.pallas import tpu as pltpu
from jax.sharding import PartitionSpec as P
import ml_dtypes

F32, BF16 = jnp.float32, jnp.bfloat16
SIDE = 128
LENGTH = 8192
BLOCKS = LENGTH // SIDE
CTX, CH = 64, 8
GROUP = 64


def led_by(first, size):
    order = list(range(size))
    order[0], order[first] = first, 0
    return order


CTX_FIRST, CH_FIRST = 53, 7
CTX_ORDER, CH_ORDER = led_by(CTX_FIRST, CTX), [7, 0, 6, 1, 5, 2, 4, 3]
LARGE = pltpu.CompilerParams(vmem_limit_bytes=20 * 1024 * 1024)
SMALL = pltpu.CompilerParams(vmem_limit_bytes=8 * 1024 * 1024)


def halves(table):
    high = table.astype(ml_dtypes.bfloat16)
    low = (table - high.astype(np.float64)).astype(ml_dtypes.bfloat16)
    return high, low


def make_tables():
    index = np.arange(SIDE)
    angle = 2.0 * np.pi / SIDE * (np.outer(index, index) % SIDE)
    waves = np.stack(halves(np.cos(angle)) + halves(np.sin(angle)))
    turn = 2.0 * np.pi / (SIDE * SIDE) * np.outer(index, index)
    twiddle = np.stack([np.cos(turn), np.sin(turn)]).astype(np.float32)
    return waves, twiddle


def split(value):
    high = value.astype(BF16)
    return high, (value - high.astype(F32)).astype(BF16)


def mul(left, right, rhs_minor=False):
    dims = (((1,), (1 if rhs_minor else 0,)), ((), ()))
    return lax.dot_general(left, right, dims, preferred_element_type=F32)


def times_table(value, table, rhs_minor=False):
    high, low = split(value)
    return (
        mul(high, table[0], rhs_minor) + mul(low, table[0], rhs_minor) + mul(high, table[1], rhs_minor)
    )


def table_times(table, value):
    high, low = split(value)
    return mul(table[0], high) + mul(table[0], low) + mul(table[1], high)


def block(rows):
    return jnp.concatenate([jnp.concatenate(row, axis=1) for row in rows], axis=0)


def turn_back(mid, twiddle):
    tc, ts = twiddle[0], twiddle[1]
    re, im = mid[:, :SIDE], mid[:, SIDE:]
    return jnp.concatenate([re * tc - im * ts, im * tc + re * ts], axis=0)


def project_kernel(tokens_hbm, weights_hbm, send_ref, weights, tokens, sems):
    half = weights.shape[1] // 2
    parts = [pl.ds(h * half, half) for h in range(2)]
    tokens_copy = pltpu.make_async_copy(tokens_hbm, tokens, sems.at[6])
    tokens_copy.start()
    blocks = [
        pltpu.make_async_copy(
            weights_hbm.at[i // 2, parts[i % 2]], weights.at[i // 2, parts[i % 2]], sems.at[i]
        )
        for i in range(6)
    ]
    for copy in blocks:
        copy.start()
    tokens_copy.wait()
    for s in range(3):
        total = None
        for h in range(2):
            blocks[2 * s + h].wait()
            part = mul(tokens[:, half * h:half * (h + 1)], weights[s, half * h:half * (h + 1)])
            total = part if total is None else total + part
        total = total.astype(BF16).T
        for k, g in enumerate(CH_ORDER):
            send_ref[k, s] = total[GROUP * g:GROUP * (g + 1)]


def swap_peers(rows_ref):
    far = pl.ds(2 * CTX_FIRST, 2)
    first, other = rows_ref[0:2], rows_ref[far]
    rows_ref[0:2] = other
    rows_ref[far] = first


def gate_kernel(parts_ref, cotangent_ref, fields_ref, send_ref, scratch):
    fields = []
    for s in range(3):
        total = parts_ref[0, s].astype(F32)
        for g in range(1, CH):
            total = total + parts_ref[g, s].astype(F32)
        rounded = total.astype(BF16)
        fields_ref[s] = rounded
        fields.append(rounded.astype(F32))
    scratch[pl.ds(0, CTX, stride=2), :] = fields[1] * fields[2]
    scratch[pl.ds(1, CTX, stride=2), :] = cotangent_ref[...].astype(F32) * fields[0]
    swap_peers(scratch)
    send_ref[...] = scratch[...].astype(BF16)


def conv_kernel(rows_ref, taps_ref, waves_ref, twiddle_ref, filter_ref, send_ref, scratch):
    cos, sin = (waves_ref[0], waves_ref[1]), (waves_ref[2], waves_ref[3])
    tc, ts = twiddle_ref[0], twiddle_ref[1]
    scratch[...] = rows_ref[...].astype(F32)
    swap_peers(scratch)
    product = scratch[pl.ds(0, CTX, stride=2), :].astype(BF16)
    conv_grad = scratch[pl.ds(1, CTX, stride=2), :].astype(BF16)
    high, low = split(taps_ref[...] * (1.0 / (math.sqrt(LENGTH) * SIDE * SIDE)))
    signals = jnp.concatenate([product, conv_grad, high], axis=1)
    signals = jnp.concatenate([signals, jnp.zeros_like(signals)], axis=0)
    outer = [jnp.concatenate([cos[i], -sin[i]], axis=0) for i in range(2)]
    first = mul(jnp.concatenate(outer, axis=1), jnp.concatenate([signals, signals], axis=0))
    rest = mul(outer[0], jnp.concatenate([low, jnp.zeros_like(low)], axis=0))
    turned = []
    for s in range(3):
        part = first[:, s * SIDE:(s + 1) * SIDE]
        if s == 2:
            part = part + rest
        re, im = part[:SIDE], part[SIDE:]
        turned.append(jnp.concatenate([re * tc + im * ts, im * tc - re * ts], axis=1))
    inner = [block([[cos[i], -sin[i]], [sin[i], cos[i]]]) for i in range(2)]
    spec = times_table(jnp.concatenate(turned, axis=0), inner)
    (pr, pi), (gr, gi), (kr, ki) = (
        (spec[s * SIDE:(s + 1) * SIDE, :SIDE], spec[s * SIDE:(s + 1) * SIDE, SIDE:])
        for s in range(3)
    )
    re = pr * kr - pi * ki - (gi * kr - gr * ki)
    im = pr * ki + pi * kr + (gr * kr + gi * ki)
    scale = 1.0 / (math.sqrt(LENGTH) * SIDE * SIDE)
    filter_re = (gr * pr + gi * pi) * scale
    filter_im = (gi * pr - gr * pi) * scale
    mid = times_table(block([[re, im], [filter_re, filter_im]]), inner, rhs_minor=True)
    back = [
        block([[cos[i][:BLOCKS], -sin[i][:BLOCKS]], [sin[i][:BLOCKS], cos[i][:BLOCKS]]])
        for i in range(2)
    ]
    both = table_times(back, turn_back(mid[:SIDE], twiddle_ref))
    scratch[pl.ds(0, CTX, stride=2), :] = both[:BLOCKS]
    scratch[pl.ds(1, CTX, stride=2), :] = both[BLOCKS:]
    swap_peers(scratch)
    send_ref[...] = scratch[...].astype(BF16)
    filter_ref[...] = table_times(
        [part[:BLOCKS] for part in back], turn_back(mid[SIDE:], twiddle_ref)
    )


def finish_kernel(
    grads_ref, gated_in_ref, filter_in_ref, weights_ref, gated_ref, input_ref, filter_ref
):
    gated_ref[...] = gated_in_ref[...]
    filter_ref[...] = filter_in_ref[...]
    total = None
    for s in range(3):
        rows = jnp.concatenate([grads_ref[CH_ORDER.index(g), s] for g in range(CH)], axis=0)
        part = mul(weights_ref[s], rows)
        total = part if total is None else total + part
    input_ref[...] = total.astype(BF16).T


def grads_kernel(rows_ref, fields_ref, cotangent_ref, send_ref, gated_ref, scratch):
    scratch[...] = rows_ref[...].astype(F32)
    swap_peers(scratch)
    convolved = scratch[pl.ds(0, CTX, stride=2), :]
    prod_grad = scratch[pl.ds(1, CTX, stride=2), :]
    query, key, value = (fields_ref[s].astype(F32) for s in range(3))
    upstream = cotangent_ref[...].astype(F32)
    gated_ref[...] = (query * convolved).astype(BF16)
    for s, row in enumerate((upstream * convolved, prod_grad * value, prod_grad * key)):
        row = row.astype(BF16)
        for k in range(CH):
            send_ref[k, s] = row


def call(kernel, shapes, scratch=(), params=SMALL, **extra):
    return pl.pallas_call(
        kernel, out_shape=shapes, compiler_params=params, scratch_shapes=list(scratch), **extra
    )


def shape(dims, dtype):
    return jax.ShapeDtypeStruct(dims, dtype)


def exchange(field, axis, order):
    return lax.all_to_all(
        field, axis, split_axis=0, concat_axis=0, tiled=True, axis_index_groups=[list(order)]
    )


def over_ctx(rows):
    return exchange(rows.reshape(CTX, 2, SIDE), "ctx", CTX_ORDER).reshape(SIDE, SIDE)


def on_device(tokens, weights, filter_taps, cotangent):
    waves, twiddle = (jnp.asarray(t) for t in make_tables())
    message = (CH, 3, GROUP, SIDE)
    parts, weights = call(
        project_kernel,
        (pltpu.VMEM(message, BF16), pltpu.VMEM(weights.shape, BF16)),
        [pltpu.VMEM(tokens.shape, BF16), pltpu.SemaphoreType.DMA((7,))],
        LARGE,
        in_specs=[pl.BlockSpec(memory_space=pltpu.HBM)] * 2,
    )(*(pltpu.with_memory_space_constraint(t, pltpu.HBM) for t in (tokens, weights)))
    parts = exchange(parts, "ch", CH_ORDER)
    fields, send = call(
        gate_kernel,
        (shape((3, GROUP, SIDE), BF16), shape((SIDE, SIDE), BF16)),
        [pltpu.VMEM((SIDE, SIDE), F32)],
    )(parts, cotangent)
    kernel_grad, send = call(
        conv_kernel,
        (shape((BLOCKS, SIDE), F32), shape((SIDE, SIDE), BF16)),
        [pltpu.VMEM((SIDE, SIDE), F32)],
    )(over_ctx(send), filter_taps.reshape(BLOCKS, SIDE), waves, twiddle)
    grads, gated = call(
        grads_kernel,
        (shape(message, BF16), shape((GROUP, SIDE), BF16)),
        [pltpu.VMEM((SIDE, SIDE), F32)],
    )(over_ctx(send), fields, cotangent)
    grads = exchange(grads, "ch", CH_ORDER)
    gated_out, input_grad, kernel_grad = call(
        finish_kernel,
        (
            shape((GROUP, SIDE), BF16),
            shape(tokens.shape, BF16),
            shape((BLOCKS, SIDE), F32),
        ),
    )(grads, gated, kernel_grad, weights)
    return gated_out, input_grad, kernel_grad.reshape(1, 1, LENGTH)


def solution(mesh):
    return jax.shard_map(
        on_device,
        mesh=mesh,
        in_specs=(P("ctx", "ch"), P(None, "ch", None), P("ctx", "ch", None), P("ch", "ctx")),
        out_specs=(P("ch", "ctx"), P("ctx", "ch"), P("ctx", "ch", None)),
        check_vma=False,
    )
```

```python
import math

import jax
import jax.numpy as jnp
import numpy as np
from jax import lax
from jax.experimental import pallas as pl
from jax.experimental.pallas import tpu as pltpu
from jax.sharding import PartitionSpec as P
import ml_dtypes

F32, BF16 = jnp.float32, jnp.bfloat16
SIDE = 128
LENGTH = 8192
BLOCKS = LENGTH // SIDE
CTX, CH = 64, 8
GROUP = 64


def led_by(first, size):
    order = list(range(size))
    order[0], order[first] = first, 0
    return order


CTX_FIRST, CH_FIRST = 55, 4
CTX_ORDER, CH_ORDER = led_by(CTX_FIRST, CTX), led_by(CH_FIRST, CH)
LARGE = pltpu.CompilerParams(vmem_limit_bytes=20 * 1024 * 1024)
SMALL = pltpu.CompilerParams(vmem_limit_bytes=8 * 1024 * 1024)


def halves(table):
    high = table.astype(ml_dtypes.bfloat16)
    low = (table - high.astype(np.float64)).astype(ml_dtypes.bfloat16)
    return high, low


def make_tables():
    index = np.arange(SIDE)
    angle = 2.0 * np.pi / SIDE * (np.outer(index, index) % SIDE)
    waves = np.stack(halves(np.cos(angle)) + halves(np.sin(angle)))
    turn = 2.0 * np.pi / (SIDE * SIDE) * np.outer(index, index)
    twiddle = np.stack([np.cos(turn), np.sin(turn)]).astype(np.float32)
    return waves, twiddle


def split(value):
    high = value.astype(BF16)
    return high, (value - high.astype(F32)).astype(BF16)


def mul(left, right, rhs_minor=False):
    dims = (((1,), (1 if rhs_minor else 0,)), ((), ()))
    return lax.dot_general(left, right, dims, preferred_element_type=F32)


def times_table(value, table, rhs_minor=False):
    high, low = split(value)
    return (
        mul(high, table[0], rhs_minor) + mul(low, table[0], rhs_minor) + mul(high, table[1], rhs_minor)
    )


def table_times(table, value):
    high, low = split(value)
    return mul(table[0], high) + mul(table[0], low) + mul(table[1], high)


def block(rows):
    return jnp.concatenate([jnp.concatenate(row, axis=1) for row in rows], axis=0)


def turn_back(mid, twiddle):
    tc, ts = twiddle[0], twiddle[1]
    re, im = mid[:, :SIDE], mid[:, SIDE:]
    return jnp.concatenate([re * tc - im * ts, im * tc + re * ts], axis=0)


def project_kernel(tokens_hbm, weights_hbm, send_ref, weights, tokens, sems):
    half = weights.shape[1] // 2
    parts = [pl.ds(h * half, half) for h in range(2)]
    tokens_copy = pltpu.make_async_copy(tokens_hbm, tokens, sems.at[6])
    tokens_copy.start()
    blocks = [
        pltpu.make_async_copy(
            weights_hbm.at[i // 2, parts[i % 2]], weights.at[i // 2, parts[i % 2]], sems.at[i]
        )
        for i in range(6)
    ]
    for copy in blocks:
        copy.start()
    tokens_copy.wait()
    for s in range(3):
        total = None
        for h in range(2):
            blocks[2 * s + h].wait()
            part = mul(tokens[:, half * h:half * (h + 1)], weights[s, half * h:half * (h + 1)])
            total = part if total is None else total + part
        total = total.astype(BF16).T
        for k, g in enumerate(CH_ORDER):
            send_ref[k, s] = total[GROUP * g:GROUP * (g + 1)]


def swap_peers(rows_ref):
    far = pl.ds(2 * CTX_FIRST, 2)
    first, other = rows_ref[0:2], rows_ref[far]
    rows_ref[0:2] = other
    rows_ref[far] = first


def gate_kernel(parts_ref, cotangent_ref, fields_ref, send_ref, scratch):
    fields = []
    for s in range(3):
        total = parts_ref[0, s].astype(F32)
        for g in range(1, CH):
            total = total + parts_ref[g, s].astype(F32)
        rounded = total.astype(BF16)
        fields_ref[s] = rounded
        fields.append(rounded.astype(F32))
    scratch[pl.ds(0, CTX, stride=2), :] = fields[1] * fields[2]
    scratch[pl.ds(1, CTX, stride=2), :] = cotangent_ref[...].astype(F32) * fields[0]
    swap_peers(scratch)
    send_ref[...] = scratch[...].astype(BF16)


def conv_kernel(rows_ref, taps_ref, waves_ref, twiddle_ref, filter_ref, send_ref, scratch):
    cos, sin = (waves_ref[0], waves_ref[1]), (waves_ref[2], waves_ref[3])
    tc, ts = twiddle_ref[0], twiddle_ref[1]
    scratch[...] = rows_ref[...].astype(F32)
    swap_peers(scratch)
    product = scratch[pl.ds(0, CTX, stride=2), :].astype(BF16)
    conv_grad = scratch[pl.ds(1, CTX, stride=2), :].astype(BF16)
    high, low = split(taps_ref[...] * (1.0 / (math.sqrt(LENGTH) * SIDE * SIDE)))
    signals = jnp.concatenate([product, conv_grad, high], axis=1)
    signals = jnp.concatenate([signals, jnp.zeros_like(signals)], axis=0)
    outer = [jnp.concatenate([cos[i], -sin[i]], axis=0) for i in range(2)]
    first = mul(jnp.concatenate(outer, axis=1), jnp.concatenate([signals, signals], axis=0))
    rest = mul(outer[0], jnp.concatenate([low, jnp.zeros_like(low)], axis=0))
    turned = []
    for s in range(3):
        part = first[:, s * SIDE:(s + 1) * SIDE]
        if s == 2:
            part = part + rest
        re, im = part[:SIDE], part[SIDE:]
        turned.append(jnp.concatenate([re * tc + im * ts, im * tc - re * ts], axis=1))
    inner = [block([[cos[i], -sin[i]], [sin[i], cos[i]]]) for i in range(2)]
    spec = times_table(jnp.concatenate(turned, axis=0), inner)
    (pr, pi), (gr, gi), (kr, ki) = (
        (spec[s * SIDE:(s + 1) * SIDE, :SIDE], spec[s * SIDE:(s + 1) * SIDE, SIDE:])
        for s in range(3)
    )
    re = pr * kr - pi * ki - (gi * kr - gr * ki)
    im = pr * ki + pi * kr + (gr * kr + gi * ki)
    scale = 1.0 / (math.sqrt(LENGTH) * SIDE * SIDE)
    filter_re = (gr * pr + gi * pi) * scale
    filter_im = (gi * pr - gr * pi) * scale
    mid = times_table(block([[re, im], [filter_re, filter_im]]), inner, rhs_minor=True)
    back = [
        block([[cos[i][:BLOCKS], -sin[i][:BLOCKS]], [sin[i][:BLOCKS], cos[i][:BLOCKS]]])
        for i in range(2)
    ]
    both = table_times(back, turn_back(mid[:SIDE], twiddle_ref))
    scratch[pl.ds(0, CTX, stride=2), :] = both[:BLOCKS]
    scratch[pl.ds(1, CTX, stride=2), :] = both[BLOCKS:]
    swap_peers(scratch)
    send_ref[...] = scratch[...].astype(BF16)
    filter_ref[...] = table_times(
        [part[:BLOCKS] for part in back], turn_back(mid[SIDE:], twiddle_ref)
    )


def finish_kernel(
    grads_ref, gated_in_ref, filter_in_ref, weights_ref, gated_ref, input_ref, filter_ref
):
    gated_ref[...] = gated_in_ref[...]
    filter_ref[...] = filter_in_ref[...]
    total = None
    for s in range(3):
        rows = jnp.concatenate([grads_ref[CH_ORDER.index(g), s] for g in range(CH)], axis=0)
        part = mul(weights_ref[s], rows)
        total = part if total is None else total + part
    input_ref[...] = total.astype(BF16).T


def grads_kernel(rows_ref, fields_ref, cotangent_ref, send_ref, gated_ref, scratch):
    scratch[...] = rows_ref[...].astype(F32)
    swap_peers(scratch)
    convolved = scratch[pl.ds(0, CTX, stride=2), :]
    prod_grad = scratch[pl.ds(1, CTX, stride=2), :]
    query, key, value = (fields_ref[s].astype(F32) for s in range(3))
    upstream = cotangent_ref[...].astype(F32)
    gated_ref[...] = (query * convolved).astype(BF16)
    for s, row in enumerate((upstream * convolved, prod_grad * value, prod_grad * key)):
        row = row.astype(BF16)
        for k in range(CH):
            send_ref[k, s] = row


def call(kernel, shapes, scratch=(), params=SMALL, **extra):
    return pl.pallas_call(
        kernel, out_shape=shapes, compiler_params=params, scratch_shapes=list(scratch), **extra
    )


def shape(dims, dtype):
    return jax.ShapeDtypeStruct(dims, dtype)


def exchange(field, axis, order):
    return lax.all_to_all(
        field, axis, split_axis=0, concat_axis=0, tiled=True, axis_index_groups=[list(order)]
    )


def over_ctx(rows):
    return exchange(rows.reshape(CTX, 2, SIDE), "ctx", CTX_ORDER).reshape(SIDE, SIDE)


def on_device(tokens, weights, filter_taps, cotangent):
    waves, twiddle = (jnp.asarray(t) for t in make_tables())
    message = (CH, 3, GROUP, SIDE)
    parts, weights = call(
        project_kernel,
        (pltpu.VMEM(message, BF16), pltpu.VMEM(weights.shape, BF16)),
        [pltpu.VMEM(tokens.shape, BF16), pltpu.SemaphoreType.DMA((7,))],
        LARGE,
        in_specs=[pl.BlockSpec(memory_space=pltpu.HBM)] * 2,
    )(*(pltpu.with_memory_space_constraint(t, pltpu.HBM) for t in (tokens, weights)))
    parts = exchange(parts, "ch", CH_ORDER)
    fields, send = call(
        gate_kernel,
        (shape((3, GROUP, SIDE), BF16), shape((SIDE, SIDE), BF16)),
        [pltpu.VMEM((SIDE, SIDE), F32)],
    )(parts, cotangent)
    kernel_grad, send = call(
        conv_kernel,
        (shape((BLOCKS, SIDE), F32), shape((SIDE, SIDE), BF16)),
        [pltpu.VMEM((SIDE, SIDE), F32)],
    )(over_ctx(send), filter_taps.reshape(BLOCKS, SIDE), waves, twiddle)
    grads, gated = call(
        grads_kernel,
        (shape(message, BF16), shape((GROUP, SIDE), BF16)),
        [pltpu.VMEM((SIDE, SIDE), F32)],
    )(over_ctx(send), fields, cotangent)
    grads = exchange(grads, "ch", CH_ORDER)
    gated_out, input_grad, kernel_grad = call(
        finish_kernel,
        (
            shape((GROUP, SIDE), BF16),
            shape(tokens.shape, BF16),
            shape((BLOCKS, SIDE), F32),
        ),
    )(grads, gated, kernel_grad, weights)
    return gated_out, input_grad, kernel_grad.reshape(1, 1, LENGTH)


def solution(mesh):
    return jax.shard_map(
        on_device,
        mesh=mesh,
        in_specs=(P("ctx", "ch"), P(None, "ch", None), P("ctx", "ch", None), P("ch", "ctx")),
        out_specs=(P("ch", "ctx"), P("ctx", "ch"), P("ctx", "ch", None)),
        check_vma=False,
    )
```
